32 devices in a mesh: ctx: 8 (over y, x, core), tp: 4 (over z).
Axes of the slice: x: 2, y: 2, z: 4, core: 2. Of those that a mesh axis runs over, the one named last changes fastest.
Arguments:
- hidden: bfloat16 [8192, 8192], P('ctx', 'tp'), may hold values from -20 to 20
- norm_gain: bfloat16 [8192], P('tp'), may hold values from 0.5 to 1.5
- router_weight: bfloat16 [8192], P('tp'), may hold values from -0.0625 to 0.0625
- query_weight: bfloat16 [8192, 4096], P('tp'), may hold values from -29 to 29
- key_value_weight: bfloat16 [2, 8192, 512], P(None, 'tp'), may hold values from -1 to 1
- out_weight: bfloat16 [4096, 8192], P(None, 'tp'), may hold values from -0.5 to 0.5
- kept_rows: int32 [8, 512], replicated, may hold values from 0 to 1024, as said below
Outputs:
- block_update: bfloat16 [8192, 8192], P('ctx', 'tp')
The draws below stay inside these ranges and needn't reach their ends.
Inputs may be any that keep to these rules, and one draw needn't show every extreme that they name: `kept_rows`: row c lists, in rising order, the distinct local indices of the kept rows of context shard c, then 1024 in every unused slot. The counts of kept rows over all shards sum to 2048; every shard keeps at least one row and some shard keeps exactly 512.
All inputs are finite; a program needn't handle non-finite values.
Results may differ from the reference program's by a relative error of at most 0.025.
Values may be sent and summed in bfloat16 or wider, within the bound.
A program may use at most 128 MiB of HBM per device.

```python
import jax
import jax.numpy as jnp
from jax import lax

D = 8192
H = 32
KVH = 4
HD = 128
TOK_DEV = 1024
KEEP_DEV = 256
CAP = 512
TOKENS = 8192
KEPT = 2048
N_CTX = 8


def shared_keys(key, bound):
    base = jax.random.normal(key, (D, KVH * HD), jnp.float32)
    return jnp.clip(base, -bound, bound) * D ** (-0.5)


def draw_hidden(key, part):
    key = jax.random.fold_in(key, 21)
    states = jnp.clip(jax.random.normal(key, (TOKENS, D), jnp.float32), -6.0, 6.0)
    return states.astype(jnp.bfloat16)


def draw_query_weight(key, part):
    key = jax.random.fold_in(key, 31)
    key_free = jax.random.fold_in(key, 0)
    weights = jnp.clip(jax.random.normal(key_free, (D, H * HD), jnp.float32), -4.0, 4.0) * D ** (-0.5)
    return weights.astype(jnp.bfloat16)


def draw_key_value_weight(key, part):
    key_weights = shared_keys(key, 4.0)
    key = jax.random.fold_in(key, 41)
    value_weights = jnp.clip(jax.random.normal(key, (D, KVH * HD), jnp.float32), -4.0, 4.0) * D ** (-0.5)
    return jnp.stack([key_weights, value_weights]).astype(jnp.bfloat16)


def draw_kept_rows(key, part):
    key = jax.random.fold_in(key, 11)
    key_weights, key_full, key_rows = jax.random.split(key, 3)
    shard_ids = jnp.arange(N_CTX, dtype=jnp.int32)
    shares = jax.random.randint(key_weights, (N_CTX,), 2, 5, dtype=jnp.int32)
    full_shard = jax.random.randint(key_full, (), 0, N_CTX, dtype=jnp.int32)
    others = jnp.where(shard_ids == full_shard, 0, shares)
    remaining = KEEP_DEV * N_CTX - CAP
    counts_base = remaining * others // jnp.sum(others)
    shortfall = remaining - jnp.sum(counts_base)
    others_rank = jnp.cumsum((others > 0).astype(jnp.int32)) - 1
    counts_base = counts_base + ((others > 0) & (others_rank < shortfall)).astype(jnp.int32)
    counts = jnp.where(shard_ids == full_shard, CAP, counts_base).astype(jnp.int32)

    def choose_rows(row_key, row_count):
        shuffled = jax.random.permutation(row_key, TOK_DEV).astype(jnp.int32)
        keep_flag = (shuffled < row_count).astype(jnp.int32)
        selected = jnp.argsort(1 - keep_flag, stable=True)[:CAP].astype(jnp.int32)
        return jnp.where(jnp.arange(CAP, dtype=jnp.int32) < row_count, selected, TOK_DEV).astype(jnp.int32)
    return jax.vmap(choose_rows)(jax.random.split(key_rows, N_CTX), counts)


def block_levels(key, shape, cuts, least, high):
    factor_of = 1.0
    for axis_at, blocks in cuts:
        steps = jax.random.uniform(jax.random.fold_in(jax.random.fold_in(key, 6), axis_at), (blocks,), jnp.float32, least / len(cuts), high / len(cuts))
        factor_of = factor_of * jnp.repeat(jnp.exp(steps), shape[axis_at] // blocks).reshape((-1,) + (1,) * (len(shape) - 1 - axis_at))
    return factor_of


def centred(stream_key, dims, width, limit, pieces=(), kind=jnp.bfloat16):
    entries = jax.random.normal(stream_key, dims, jnp.float32) * width
    if len(pieces) > 0:
        entries = block_levels(stream_key, dims, pieces, -0.22, 0.18) * entries
    return jnp.clip(entries, min=-limit, max=limit).astype(kind)


def setup_inputs(seed: int = 0) -> dict:
    seeds = jax.random.split(jax.random.key(seed), 8)
    hidden = draw_hidden(jax.random.fold_in(seeds[7], 71), 0)
    norm_gain = jnp.clip(1.0 + 0.1 * jax.random.normal(seeds[1], (D,), jnp.float32), 0.5, 1.5).astype(jnp.bfloat16)
    router_weight = centred(seeds[2], (D,), D ** -0.5, 0.0625, ((0, 4),))
    query_weight = draw_query_weight(jax.random.fold_in(seeds[7], 71), 0)
    key_value_weight = draw_key_value_weight(jax.random.fold_in(seeds[7], 71), 0)
    out_weight = centred(seeds[5], (H * HD, D), HD ** -0.5, 0.5, ((1, 4),))
    kept_rows = draw_kept_rows(jax.random.fold_in(seeds[7], 71), 0)
    return dict(hidden=hidden, norm_gain=norm_gain, router_weight=router_weight, query_weight=query_weight, key_value_weight=key_value_weight, out_weight=out_weight, kept_rows=kept_rows)


EPSILON = 1e-05
MASKED_SCORE = -1e+30

def reference(hidden, norm_gain, router_weight, query_weight, key_value_weight, out_weight, kept_rows):
    shard_ids = jnp.arange(N_CTX, dtype=jnp.int32)[:, None]
    flat_positions = jnp.where(kept_rows < TOK_DEV, shard_ids * TOK_DEV + kept_rows, TOKENS).reshape(-1)
    positions = jnp.sort(flat_positions)[:KEPT].astype(jnp.int32)
    kept_states = hidden[positions]
    widened = kept_states.astype(jnp.float32)
    square_sum = lax.optimization_barrier(jnp.sum(widened * widened, axis=1))
    router_logit = jnp.dot(kept_states, router_weight, preferred_element_type=jnp.float32)
    normed = (widened * norm_gain.astype(jnp.float32)).astype(jnp.bfloat16)
    inverse_rms = lax.rsqrt(square_sum / D + EPSILON)
    queries = (jnp.dot(normed, query_weight, preferred_element_type=jnp.float32) * inverse_rms[:, None]).astype(jnp.bfloat16)
    keys = (jnp.dot(normed, key_value_weight[0], preferred_element_type=jnp.float32) * inverse_rms[:, None]).astype(jnp.bfloat16)
    values = (jnp.dot(normed, key_value_weight[1], preferred_element_type=jnp.float32) * inverse_rms[:, None]).astype(jnp.bfloat16)
    queries = queries.reshape(KEPT, H, HD)
    keys = keys.reshape(KEPT, KVH, HD)
    values = values.reshape(KEPT, KVH, HD)
    allowed = positions[None, :] <= positions[:, None]
    score_scale = HD ** (-0.5)

    def one_head(head_id):
        group_id = head_id // (H // KVH)
        query_head = lax.dynamic_index_in_dim(queries, head_id, 1, keepdims=False)
        key_head = lax.dynamic_index_in_dim(keys, group_id, 1, keepdims=False)
        value_head = lax.dynamic_index_in_dim(values, group_id, 1, keepdims=False)
        scores = jnp.dot(query_head, key_head.T, preferred_element_type=jnp.float32) * score_scale
        scores = jnp.where(allowed, scores, MASKED_SCORE)
        peak = lax.optimization_barrier(jnp.max(scores, axis=1, keepdims=True))
        weights = jnp.where(allowed, jnp.exp(scores - peak), 0.0)
        total = lax.optimization_barrier(jnp.sum(weights, axis=1))
        mixed = jnp.dot(weights.astype(jnp.bfloat16), value_head, preferred_element_type=jnp.float32)
        return (mixed / total[:, None]).astype(jnp.bfloat16)
    head_output = lax.map(one_head, jnp.arange(H, dtype=jnp.int32))
    head_output = jnp.transpose(head_output, (1, 0, 2)).reshape(KEPT, H * HD)
    projected = jnp.dot(head_output, out_weight, preferred_element_type=jnp.float32)
    row_update = (jax.nn.sigmoid(router_logit)[:, None] * projected).astype(jnp.bfloat16)
    return jnp.zeros_like(hidden).at[positions].set(row_update)
```

```python
import functools

import jax
import jax.numpy as jnp
from jax import lax
from jax.experimental import pallas as pl
from jax.experimental.pallas import tpu as pltpu
from jax.sharding import PartitionSpec as P

D = 8192
H = 32
KVH = 4
HD = 128
EPSILON = 1e-05
MASKED_SCORE = -1e30
BF16 = jnp.bfloat16
F32 = jnp.float32


def attention_kernel(ctx_count, keep, q_ref, k_ref, v_ref, me_ref, o_ref):
    heads = q_ref.shape[1] // HD
    me = me_ref[0]
    rows = keep // 2
    for half in range(2):
        span = rows * (half + 1)
        q_rank = (lax.broadcasted_iota(jnp.int32, (rows, span), 0) + half * rows) * ctx_count + me
        slot = lax.broadcasted_iota(jnp.int32, (rows, span), 1) * ctx_count
        masks = [slot + c <= q_rank for c in range(ctx_count)]
        for h in range(heads):
            q = q_ref[pl.ds(half * rows, rows), pl.ds(h * HD, HD)]
            scores = []
            for c in range(ctx_count):
                s = lax.dot_general(
                    q, k_ref[c, pl.ds(0, span), :], (((1,), (1,)), ((), ())),
                    preferred_element_type=F32,
                ) * (HD ** -0.5)
                scores.append(jnp.where(masks[c], s, MASKED_SCORE))
            peak = functools.reduce(jnp.maximum, scores)
            peak = jnp.max(peak, axis=1, keepdims=True)
            total = jnp.zeros((rows, span), F32)
            mixed = jnp.zeros((rows, HD), F32)
            for c in range(ctx_count):
                w = jnp.exp(scores[c] - peak)
                total = total + w
                mixed = mixed + jnp.dot(
                    w.astype(BF16), v_ref[c, pl.ds(0, span), :], preferred_element_type=F32
                )
            total = jnp.sum(total, axis=1, keepdims=True)
            o_ref[pl.ds(half * rows, rows), pl.ds(h * HD, HD)] = (mixed / total).astype(BF16)


def attention(q, k, v, me, ctx_count, keep):
    return pl.pallas_call(
        functools.partial(attention_kernel, ctx_count, keep),
        out_shape=jax.ShapeDtypeStruct(q.shape, BF16),
        in_specs=[pl.BlockSpec(memory_space=pltpu.VMEM)] * 3
        + [pl.BlockSpec(memory_space=pltpu.SMEM)],
        out_specs=pl.BlockSpec(memory_space=pltpu.VMEM),
        compiler_params=pltpu.CompilerParams(vmem_limit_bytes=48 * 2**20),
        name="attention",
    )(q, k, v, me)


def one_hot(index, count, axis):
    shape = (count,) + index.shape if axis == 0 else index.shape + (count,)
    iota = lax.broadcasted_iota(jnp.int32, shape, 0 if axis == 0 else len(shape) - 1)
    target = index[None] if axis == 0 else index[..., None]
    return (iota == target).astype(BF16)


def shards(hidden, norm_gain, router_weight, query_weight, key_value_weight, out_weight, kept_rows):
    me = lax.axis_index("ctx")
    ctx_count = lax.axis_size("ctx")
    tp_count = lax.axis_size("tp")
    tp_index = lax.axis_index("tp")
    token_count, width = hidden.shape
    capacity = kept_rows.shape[1]
    keep = capacity // 2
    part = capacity // ctx_count
    heads = H // tp_count

    counts = jnp.sum((kept_rows < token_count).astype(jnp.int32), axis=1)
    starts = jnp.cumsum(counts) - counts
    ids = jnp.arange(ctx_count, dtype=jnp.int32)
    slots = jnp.arange(part, dtype=jnp.int32)

    first = (ids - starts[me]) % ctx_count
    send_index = first[:, None] + ctx_count * slots[None, :]
    own_rows = lax.dynamic_index_in_dim(kept_rows, me, 0, keepdims=False)
    send_rows = jnp.take(own_rows, send_index.reshape(-1), axis=0)
    pick = one_hot(send_rows, token_count, 1)
    sent = jnp.dot(pick, hidden, preferred_element_type=F32).astype(BF16)
    got = lax.all_to_all(sent.reshape(ctx_count, part, width), "ctx", 0, 0).reshape(capacity, width)

    come_first = (me - starts) % ctx_count
    come_slot = (starts + come_first)[:, None] // ctx_count + slots[None, :]
    come_valid = come_first[:, None] + ctx_count * slots[None, :] < counts[:, None]
    place = jnp.where(come_valid, come_slot, keep).reshape(-1)
    compact = one_hot(place, keep, 0)
    kept = jnp.dot(compact, got, preferred_element_type=F32).astype(BF16)

    widened = kept.astype(F32)
    square_part = jnp.sum(widened * widened, axis=1)
    router_part = jnp.dot(kept, router_weight, preferred_element_type=F32)
    normed = (widened * norm_gain.astype(F32)).astype(BF16)
    square_sum, router_logit = lax.psum((square_part, router_part), "tp")
    inverse_rms = lax.rsqrt(square_sum / D + EPSILON)

    q_terms = lax.dot_general(
        query_weight, normed, (((0,), (1,)), ((), ())), preferred_element_type=F32
    ).astype(BF16).reshape(tp_count, heads * HD, keep)
    kv_terms = lax.dot_general(
        key_value_weight, normed, (((1,), (1,)), ((), ())), preferred_element_type=F32
    ).astype(BF16).reshape(2, KVH, HD, keep)
    group_of = [t * heads // (H // KVH) for t in range(tp_count)]
    kv_terms = jnp.stack([kv_terms[:, g] for g in group_of]).reshape(tp_count, 2 * HD, keep)
    terms = jnp.concatenate([q_terms, kv_terms], axis=1)
    sums = lax.psum_scatter(terms, "tp", scatter_dimension=0, tiled=False)
    scaled = (sums.astype(F32) * inverse_rms[None, :]).astype(BF16).T
    queries = scaled[:, : heads * HD]
    key_values = lax.all_gather(scaled[:, heads * HD :], "ctx", axis=0, tiled=False)
    head_output = attention(
        queries, key_values[:, :, :HD], key_values[:, :, HD:], me.reshape(1), ctx_count, keep
    )

    gathered = lax.all_gather(head_output, "tp", axis=0, tiled=False)
    projected = jnp.einsum(
        "tqe,tef->qf", gathered, out_weight.reshape(tp_count, heads * HD, width),
        preferred_element_type=F32,
    )
    row_update = (jax.nn.sigmoid(router_logit)[:, None] * projected).astype(BF16)

    back = lax.dot_general(
        compact, row_update, (((0,), (0,)), ((), ())), preferred_element_type=F32
    ).astype(BF16)
    home = lax.all_to_all(back.reshape(ctx_count, part, width), "ctx", 0, 0).reshape(capacity, width)
    return lax.dot_general(
        pick, home, (((0,), (0,)), ((), ())), preferred_element_type=F32
    ).astype(BF16)


def solution(mesh):
    return jax.shard_map(
        shards,
        mesh=mesh,
        in_specs=(
            P("ctx", "tp"),
            P("tp"),
            P("tp"),
            P("tp", None),
            P(None, "tp", None),
            P(None, "tp"),
            P(),
        ),
        out_specs=P("ctx", "tp"),
        check_vma=False,
    )
```

```python
import functools

import jax
import jax.numpy as jnp
from jax import lax
from jax.experimental import pallas as pl
from jax.experimental.pallas import tpu as pltpu
from jax.sharding import PartitionSpec as P

D = 8192
H = 32
KVH = 4
HD = 128
EPSILON = 1e-05
MASKED_SCORE = -1e30
BF16 = jnp.bfloat16
F32 = jnp.float32


MESH = pl.DeviceIdType.MESH
ROWS = 256
WIDE = 2 * HD
KV_CHUNKS = 2
Q_CHUNKS = H // 4
CHUNKS = KV_CHUNKS + Q_CHUNKS


def greet(ctx_partners, tp_partners):
    barrier = pltpu.get_barrier_semaphore()
    for c in ctx_partners:
        pl.semaphore_signal(barrier, inc=1, device_id={"ctx": c}, device_id_type=MESH)
    for t in tp_partners:
        pl.semaphore_signal(barrier, inc=1, device_id={"tp": t}, device_id_type=MESH)
    pl.semaphore_wait(barrier, len(ctx_partners) + len(tp_partners))


def project_kernel(
    ctx_count, tp_count, x_ref, stats_ref, wq_ref, wkv_ref, q_ref, kv_ref, logit_ref,
    weights, sent, got, stats, scale, weight_sem, send_sem, recv_sem,
    stat_send, stat_recv, kv_send, kv_recv, pair_send, pair_recv,
):
    me, z = lax.axis_index("ctx"), lax.axis_index("tp")
    last = tp_count - 1
    twin = me + 1 - 2 * (me % 2)
    peers = [(me + 2 * k) % ctx_count for k in range(1, ctx_count // 2)]
    others = [(z + k) % tp_count for k in range(1, tp_count)]

    def weight_copy(half, i):
        columns = pl.ds(half * WIDE, WIDE)
        if i < KV_CHUNKS:
            source = wkv_ref.at[i, :, columns]
        else:
            source = wq_ref.at[:, pl.ds((half * Q_CHUNKS + i - KV_CHUNKS) * WIDE, WIDE)]
        return pltpu.make_async_copy(source, weights.at[half, i], weight_sem.at[half, i])

    for i in range(CHUNKS):
        for half in (1, 0):
            weight_copy(half, i).start()

    greet(peers + [twin], others)

    def stat_copy(k):
        return pltpu.make_async_remote_copy(
            src_ref=stats_ref, dst_ref=stats.at[z], send_sem=stat_send.at[k],
            recv_sem=stat_recv.at[k], device_id={"tp": others[k]}, device_id_type=MESH,
        )

    for k in range(tp_count - 1):
        stat_copy(k).start()

    def kv_copy(k, part):
        return pltpu.make_async_remote_copy(
            src_ref=kv_ref.at[me, part], dst_ref=kv_ref.at[me, part],
            send_sem=kv_send.at[k, part], recv_sem=kv_recv.at[k, part],
            device_id={"ctx": peers[k]}, device_id_type=MESH,
        )

    def pair_copy(k):
        origin = (me + ctx_count - 2 * k) % ctx_count
        return pltpu.make_async_remote_copy(
            src_ref=kv_ref.at[origin], dst_ref=kv_ref.at[origin],
            send_sem=pair_send.at[k], recv_sem=pair_recv.at[k],
            device_id={"ctx": twin}, device_id_type=MESH,
        )

    def chain(half, i):
        target = jnp.minimum(z + 1, last) if half == 1 else jnp.maximum(z - 1, 0)
        return pltpu.make_async_remote_copy(
            src_ref=sent.at[half, i], dst_ref=got.at[half, i],
            send_sem=send_sem.at[half, i], recv_sem=recv_sem.at[half, i],
            device_id={"tp": target}, device_id_type=MESH,
        )

    at_first = (z == last, z == 0)
    at_final = (z == 0, z == last)

    stats[z] = stats_ref[...]
    for k in range(tp_count - 1):
        stat_copy(k).wait()
    total = stats[0]
    for t in range(1, tp_count):
        total = total + stats[t]
    inverse = lax.rsqrt(total[0:1] / D + EPSILON)
    scale[...] = jnp.broadcast_to(inverse, (WIDE, ROWS)).T
    logit_ref[...] = jnp.broadcast_to(total[1:2], (HD, ROWS)).T

    def step(i, carry):
        for half in (1, 0):
            pltpu.make_async_copy(
                wkv_ref.at[0, :, pl.ds(0, WIDE)], weights.at[half, i], weight_sem.at[half, i]
            ).wait()
            term = jnp.dot(x_ref[...], weights[half, i], preferred_element_type=F32)
            sent[half, i] = term.astype(BF16)

            @pl.when(jnp.logical_not(at_first[half]))
            def _():
                chain(half, i).wait_recv()
                sent[half, i] = (term + got[half, i].astype(F32)).astype(BF16)

            @pl.when(jnp.logical_not(at_final[half]))
            def _():
                chain(half, i).start()

            @pl.when(at_final[half])
            def _():
                done = ((term + got[half, i].astype(F32)) * scale[...]).astype(BF16)

                @pl.when(i < KV_CHUNKS)
                def _():
                    part = jnp.minimum(i, KV_CHUNKS - 1)
                    kv_ref[me, part] = done
                    for k in range(len(peers)):
                        kv_copy(k, part).start()

                @pl.when(i >= KV_CHUNKS)
                def _():
                    q_ref[jnp.maximum(i - KV_CHUNKS, 0)] = done

        return carry

    lax.fori_loop(0, CHUNKS, step, 0)

    @pl.when(jnp.logical_or(z == 0, z == last))
    def _():
        pair_copy(0).start()
        for k in range(len(peers)):
            for part in range(KV_CHUNKS):
                kv_copy(k, part).wait()
            pair_copy(k + 1).start()
        for k in range(len(peers) + 1):
            pair_copy(k).wait()

    for half in (0, 1):
        @pl.when(jnp.logical_not(at_final[half]))
        def _():
            for i in range(CHUNKS):
                chain(half, i).wait_send()


def project(normed, stats, query_weight, key_value_weight, ctx_count, tp_count):
    width = normed.shape[1]
    vmem = pl.BlockSpec(memory_space=pltpu.VMEM)
    hbm = pl.BlockSpec(memory_space=pl.ANY)
    dma = pltpu.SemaphoreType.DMA
    return pl.pallas_call(
        functools.partial(project_kernel, ctx_count, tp_count),
        out_shape=(
            jax.ShapeDtypeStruct((Q_CHUNKS, ROWS, WIDE), BF16),
            jax.ShapeDtypeStruct((ctx_count, KV_CHUNKS, ROWS, WIDE), BF16),
            jax.ShapeDtypeStruct((ROWS, HD), F32),
        ),
        in_specs=[vmem, vmem, hbm, hbm],
        out_specs=(vmem, vmem, vmem),
        scratch_shapes=[
            pltpu.VMEM((2, CHUNKS, width, WIDE), BF16),
            pltpu.VMEM((2, CHUNKS, ROWS, WIDE), BF16),
            pltpu.VMEM((2, CHUNKS, ROWS, WIDE), BF16),
            pltpu.VMEM((tp_count, 8, ROWS), F32),
            pltpu.VMEM((ROWS, WIDE), F32),
            dma((2, CHUNKS)),
            dma((2, CHUNKS)),
            dma((2, CHUNKS)),
            dma((tp_count - 1,)),
            dma((tp_count - 1,)),
            dma((ctx_count // 2 - 1, KV_CHUNKS)),
            dma((ctx_count // 2 - 1, KV_CHUNKS)),
            dma((ctx_count // 2,)),
            dma((ctx_count // 2,)),
        ],
        compiler_params=pltpu.CompilerParams(
            collective_id=0, has_side_effects=True, vmem_limit_bytes=52 * 2**20
        ),
        name="project_and_sum",
    )(normed, stats, query_weight, key_value_weight)


def attend_kernel(
    ctx_count, tp_count, q_ref, kv_ref, logit_ref, wo_ref, o_ref,
    weights, heads, acc, weight_sem, send_sem, recv_sem,
):
    me, z = lax.axis_index("ctx"), lax.axis_index("tp")
    last = tp_count - 1

    def weight_copy(half, i):
        rows = pl.ds((half * Q_CHUNKS + i) * WIDE, WIDE)
        return pltpu.make_async_copy(wo_ref.at[rows, :], weights.at[half, i], weight_sem.at[half, i])

    for i in range(Q_CHUNKS):
        for half in (0, 1):
            weight_copy(half, i).start()

    greet([], [(z + k) % tp_count for k in range(1, tp_count)])

    def chain(half, i):
        target = jnp.minimum(z + 1, last) if half == 0 else jnp.maximum(z - 1, 0)
        return pltpu.make_async_remote_copy(
            src_ref=heads.at[half, i], dst_ref=heads.at[half, i],
            send_sem=send_sem.at[half, i], recv_sem=recv_sem.at[half, i],
            device_id={"tp": target}, device_id_type=MESH,
        )

    at_first = (z == 0, z == last)
    at_final = (z == last, z == 0)
    acc[...] = jnp.zeros_like(acc)

    def multiply(half, i):
        weight_copy(half, i).wait()
        acc[...] += jnp.dot(heads[half, i], weights[half, i], preferred_element_type=F32)

    def attend(half, i):
        column = pl.ds(pl.multiple_of(i // (Q_CHUNKS // 2) * HD, HD), HD)
        rows = ROWS // 2
        for block in range(2):
            span = rows * (block + 1)
            q_rank = (lax.broadcasted_iota(jnp.int32, (rows, span), 0) + block * rows) * ctx_count + me
            q_rank = jnp.concatenate([q_rank, q_rank], axis=0)
            slot = lax.broadcasted_iota(jnp.int32, (2 * rows, span), 1) * ctx_count
            q = q_ref[i, pl.ds(block * rows, rows), :]
            q = jnp.concatenate([q[:, :HD], q[:, HD:]], axis=0)
            scores = []
            for c in range(ctx_count):
                s = lax.dot_general(
                    q, kv_ref[c, 0, pl.ds(0, span), column], (((1,), (1,)), ((), ())),
                    preferred_element_type=F32,
                ) * (HD ** -0.5)
                scores.append(jnp.where(slot + c <= q_rank, s, MASKED_SCORE))
            peak = jnp.max(functools.reduce(jnp.maximum, scores), axis=1, keepdims=True)
            total = jnp.zeros((2 * rows, span), F32)
            mixed = jnp.zeros((2 * rows, HD), F32)
            for c in range(ctx_count):
                w = jnp.exp(scores[c] - peak)
                total = total + w
                mixed = mixed + jnp.dot(
                    w.astype(BF16), kv_ref[c, 1, pl.ds(0, span), column], preferred_element_type=F32
                )
            result = (mixed / jnp.sum(total, axis=1, keepdims=True)).astype(BF16)
            here = pl.ds(block * rows, rows)
            heads[half, i, here, :] = jnp.concatenate([result[:rows], result[rows:]], axis=1)

    for half in (0, 1):
        @pl.when(at_first[half])
        def _():
            def own(i, carry):
                attend(half, i)
                chain(half, i).start()
                multiply(half, i)
                return carry

            lax.fori_loop(0, Q_CHUNKS, own, 0)

    def rest(i, carry):
        for half in (0, 1):
            @pl.when(jnp.logical_not(at_first[half]))
            def _():
                chain(half, i).wait_recv()

                @pl.when(jnp.logical_not(at_final[half]))
                def _():
                    chain(half, i).start()

                multiply(half, i)

        return carry

    lax.fori_loop(0, Q_CHUNKS, rest, 0)
    gate = jax.nn.sigmoid(logit_ref[:, 0:1])
    o_ref[...] = (gate * acc[...]).astype(BF16)

    for half in (0, 1):
        @pl.when(jnp.logical_not(at_final[half]))
        def _():
            for i in range(Q_CHUNKS):
                chain(half, i).wait_send()


def attend_and_project(queries, key_values, logit, out_weight, ctx_count, tp_count):
    width = out_weight.shape[1]
    vmem = pl.BlockSpec(memory_space=pltpu.VMEM)
    dma = pltpu.SemaphoreType.DMA
    return pl.pallas_call(
        functools.partial(attend_kernel, ctx_count, tp_count),
        out_shape=jax.ShapeDtypeStruct((ROWS, width), BF16),
        in_specs=[vmem, vmem, vmem, pl.BlockSpec(memory_space=pl.ANY)],
        out_specs=vmem,
        scratch_shapes=[
            pltpu.VMEM((2, Q_CHUNKS, WIDE, width), BF16),
            pltpu.VMEM((2, Q_CHUNKS, ROWS, WIDE), BF16),
            pltpu.VMEM((ROWS, width), F32),
            dma((2, Q_CHUNKS)),
            dma((2, Q_CHUNKS)),
            dma((2, Q_CHUNKS)),
        ],
        compiler_params=pltpu.CompilerParams(
            collective_id=1, has_side_effects=True, vmem_limit_bytes=52 * 2**20
        ),
        name="attend_and_project",
    )(queries, key_values, logit, out_weight)


def one_hot(index, count, axis):
    shape = (count,) + index.shape if axis == 0 else index.shape + (count,)
    iota = lax.broadcasted_iota(jnp.int32, shape, 0 if axis == 0 else len(shape) - 1)
    target = index[None] if axis == 0 else index[..., None]
    return (iota == target).astype(BF16)


def shards(hidden, norm_gain, router_weight, query_weight, key_value_weight, out_weight, kept_rows):
    me = lax.axis_index("ctx")
    ctx_count = lax.axis_size("ctx")
    tp_count = lax.axis_size("tp")
    token_count, width = hidden.shape
    capacity = kept_rows.shape[1]
    keep = capacity // 2
    part = capacity // ctx_count

    counts = jnp.sum((kept_rows < token_count).astype(jnp.int32), axis=1)
    starts = jnp.cumsum(counts) - counts
    ids = jnp.arange(ctx_count, dtype=jnp.int32)
    slots = jnp.arange(part, dtype=jnp.int32)

    first = (ids - starts[me]) % ctx_count
    send_index = first[:, None] + ctx_count * slots[None, :]
    own_rows = lax.dynamic_index_in_dim(kept_rows, me, 0, keepdims=False)
    send_rows = jnp.take(own_rows, send_index.reshape(-1), axis=0)
    pick = one_hot(send_rows, token_count, 1)
    sent = jnp.dot(pick, hidden, preferred_element_type=F32).astype(BF16)
    got = lax.all_to_all(sent.reshape(ctx_count, part, width), "ctx", 0, 0).reshape(capacity, width)

    come_first = (me - starts) % ctx_count
    come_slot = (starts + come_first)[:, None] // ctx_count + slots[None, :]
    come_valid = come_first[:, None] + ctx_count * slots[None, :] < counts[:, None]
    place = jnp.where(come_valid, come_slot, keep).reshape(-1)
    compact = one_hot(place, keep, 0)
    kept = jnp.dot(compact, got, preferred_element_type=F32).astype(BF16)

    widened = kept.astype(F32)
    square_part = jnp.sum(widened * widened, axis=1)
    router_part = jnp.dot(kept, router_weight, preferred_element_type=F32)
    normed = (widened * norm_gain.astype(F32)).astype(BF16)
    stats = jnp.pad(jnp.stack([square_part, router_part]), ((0, 6), (0, 0)))
    queries, key_values, logit = project(
        normed, stats, query_weight, key_value_weight, ctx_count, tp_count
    )
    row_update = attend_and_project(queries, key_values, logit, out_weight, ctx_count, tp_count)

    back = lax.dot_general(
        compact, row_update, (((0,), (0,)), ((), ())), preferred_element_type=F32
    ).astype(BF16)
    home = lax.all_to_all(back.reshape(ctx_count, part, width), "ctx", 0, 0).reshape(capacity, width)
    return lax.dot_general(
        pick, home, (((0,), (0,)), ((), ())), preferred_element_type=F32
    ).astype(BF16)


def solution(mesh):
    return jax.shard_map(
        shards,
        mesh=mesh,
        in_specs=(
            P("ctx", "tp"),
            P("tp"),
            P("tp"),
            P("tp", None),
            P(None, "tp", None),
            P(None, "tp"),
            P(),
        ),
        out_specs=P("ctx", "tp"),
        check_vma=False,
    )
```

```python
import functools

import jax
import jax.numpy as jnp
from jax import lax
from jax.experimental import pallas as pl
from jax.experimental.pallas import tpu as pltpu
from jax.sharding import PartitionSpec as P

D = 8192
H = 32
KVH = 4
HD = 128
EPSILON = 1e-05
MASKED_SCORE = -1e30
BF16 = jnp.bfloat16
F32 = jnp.float32


def attention_kernel(ctx_count, keep, q_ref, k_ref, v_ref, me_ref, o_ref):
    heads = q_ref.shape[1] // HD
    me = me_ref[0]
    rows = keep // 2
    for half in range(2):
        span = rows * (half + 1)
        q_rank = (lax.broadcasted_iota(jnp.int32, (rows, span), 0) + half * rows) * ctx_count + me
        slot = lax.broadcasted_iota(jnp.int32, (rows, span), 1) * ctx_count
        masks = [slot + c <= q_rank for c in range(ctx_count)]
        for h in range(heads):
            q = q_ref[pl.ds(half * rows, rows), pl.ds(h * HD, HD)]
            scores = []
            for c in range(ctx_count):
                s = lax.dot_general(
                    q, k_ref[c, pl.ds(0, span), :], (((1,), (1,)), ((), ())),
                    preferred_element_type=F32,
                ) * (HD ** -0.5)
                scores.append(jnp.where(masks[c], s, MASKED_SCORE))
            peak = functools.reduce(jnp.maximum, scores)
            peak = jnp.max(peak, axis=1, keepdims=True)
            total = jnp.zeros((rows, span), F32)
            mixed = jnp.zeros((rows, HD), F32)
            for c in range(ctx_count):
                w = jnp.exp(scores[c] - peak)
                total = total + w
                mixed = mixed + jnp.dot(
                    w.astype(BF16), v_ref[c, pl.ds(0, span), :], preferred_element_type=F32
                )
            total = jnp.sum(total, axis=1, keepdims=True)
            o_ref[pl.ds(half * rows, rows), pl.ds(h * HD, HD)] = (mixed / total).astype(BF16)


def attention(q, k, v, me, ctx_count, keep):
    return pl.pallas_call(
        functools.partial(attention_kernel, ctx_count, keep),
        out_shape=jax.ShapeDtypeStruct(q.shape, BF16),
        in_specs=[pl.BlockSpec(memory_space=pltpu.VMEM)] * 3
        + [pl.BlockSpec(memory_space=pltpu.SMEM)],
        out_specs=pl.BlockSpec(memory_space=pltpu.VMEM),
        compiler_params=pltpu.CompilerParams(vmem_limit_bytes=48 * 2**20),
        name="attention",
    )(q, k, v, me)


def one_hot(index, count, axis):
    shape = (count,) + index.shape if axis == 0 else index.shape + (count,)
    iota = lax.broadcasted_iota(jnp.int32, shape, 0 if axis == 0 else len(shape) - 1)
    target = index[None] if axis == 0 else index[..., None]
    return (iota == target).astype(BF16)


def shards(hidden, norm_gain, router_weight, query_weight, key_value_weight, out_weight, kept_rows):
    me = lax.axis_index("ctx")
    ctx_count = lax.axis_size("ctx")
    tp_count = lax.axis_size("tp")
    tp_index = lax.axis_index("tp")
    token_count, width = hidden.shape
    capacity = kept_rows.shape[1]
    keep = capacity // 2
    part = capacity // ctx_count
    heads = H // tp_count

    counts = jnp.sum((kept_rows < token_count).astype(jnp.int32), axis=1)
    starts = jnp.cumsum(counts) - counts
    ids = jnp.arange(ctx_count, dtype=jnp.int32)
    slots = jnp.arange(part, dtype=jnp.int32)

    first = (ids - starts[me]) % ctx_count
    send_index = first[:, None] + ctx_count * slots[None, :]
    own_rows = lax.dynamic_index_in_dim(kept_rows, me, 0, keepdims=False)
    send_rows = jnp.take(own_rows, send_index.reshape(-1), axis=0)
    pick = one_hot(send_rows, token_count, 1)
    sent = jnp.dot(pick, hidden, preferred_element_type=F32).astype(BF16)
    got = lax.all_to_all(sent.reshape(ctx_count, part, width), "ctx", 0, 0).reshape(capacity, width)

    come_first = (me - starts) % ctx_count
    come_slot = (starts + come_first)[:, None] // ctx_count + slots[None, :]
    come_valid = come_first[:, None] + ctx_count * slots[None, :] < counts[:, None]
    place = jnp.where(come_valid, come_slot, keep).reshape(-1)
    compact = one_hot(place, keep, 0)
    kept = jnp.dot(compact, got, preferred_element_type=F32).astype(BF16)

    widened = kept.astype(F32)
    square_part = jnp.sum(widened * widened, axis=1)
    router_part = jnp.dot(kept, router_weight, preferred_element_type=F32)
    normed = (widened * norm_gain.astype(F32)).astype(BF16)

    pieces = []
    remainder = jnp.stack([square_part, router_part])
    for _ in range(3):
        piece = lax.reduce_precision(remainder, 8, 7)
        pieces.append(piece.astype(BF16))
        remainder = remainder - piece
    own_slot = (jnp.arange(tp_count) == tp_index)[:, None, None]
    stat_terms = jnp.where(own_slot, jnp.concatenate(pieces)[None], 0).reshape(6 * tp_count, keep)
    stat_terms = jnp.broadcast_to(stat_terms[None], (tp_count,) + stat_terms.shape)

    kv_terms = lax.dot_general(
        key_value_weight, normed, (((1,), (1,)), ((), ())), preferred_element_type=F32
    ).astype(BF16).reshape(2, KVH, HD, keep)
    group_of = [t * heads // (H // KVH) for t in range(tp_count)]
    kv_terms = jnp.stack([kv_terms[:, g] for g in group_of]).reshape(tp_count, 2 * HD, keep)
    kv_sums = lax.psum_scatter(
        jnp.concatenate([kv_terms, stat_terms], axis=1), "tp", scatter_dimension=0, tiled=False
    )
    q_terms = lax.dot_general(
        query_weight, normed, (((0,), (1,)), ((), ())), preferred_element_type=F32
    ).astype(BF16)
    q_sums = lax.psum_scatter(q_terms, "tp", scatter_dimension=0, tiled=True)

    stats = jnp.sum(kv_sums[2 * HD :].astype(F32).reshape(tp_count * 3, 2, keep), axis=0)
    inverse_rms = lax.rsqrt(stats[0] / D + EPSILON)
    router_logit = stats[1]
    key_values = (kv_sums[: 2 * HD].astype(F32) * inverse_rms[None, :]).astype(BF16).T
    key_values = lax.all_to_all(
        jnp.broadcast_to(key_values[None], (ctx_count,) + key_values.shape), "ctx", 0, 0
    )
    queries = (q_sums.astype(F32) * inverse_rms[None, :]).astype(BF16).T

    batches = 2
    size = heads // batches * HD
    weight = out_weight.reshape(tp_count, batches, size, width)
    projected = 0.0
    for b in range(batches):
        head_output = attention(
            queries[:, b * size : (b + 1) * size], key_values[:, :, :HD], key_values[:, :, HD:],
            me.reshape(1), ctx_count, keep,
        )
        gathered = lax.all_gather(head_output, "tp", axis=0, tiled=False)
        projected = projected + jnp.einsum(
            "tqe,tef->qf", gathered, weight[:, b], preferred_element_type=F32
        )
    row_update = (jax.nn.sigmoid(router_logit)[:, None] * projected).astype(BF16)

    back = lax.dot_general(
        compact, row_update, (((0,), (0,)), ((), ())), preferred_element_type=F32
    ).astype(BF16)
    home = lax.all_to_all(back.reshape(ctx_count, part, width), "ctx", 0, 0).reshape(capacity, width)
    return lax.dot_general(
        pick, home, (((0,), (0,)), ((), ())), preferred_element_type=F32
    ).astype(BF16)


def solution(mesh):
    return jax.shard_map(
        shards,
        mesh=mesh,
        in_specs=(
            P("ctx", "tp"),
            P("tp"),
            P("tp"),
            P("tp", None),
            P(None, "tp", None),
            P(None, "tp"),
            P(),
        ),
        out_specs=P("ctx", "tp"),
        check_vma=False,
    )
```

```python
import functools

import jax
import jax.numpy as jnp
from jax import lax
from jax.experimental import pallas as pl
from jax.experimental.pallas import tpu as pltpu
from jax.sharding import PartitionSpec as P

D = 8192
H = 32
KVH = 4
HD = 128
EPSILON = 1e-05
MASKED_SCORE = -1e30
BF16 = jnp.bfloat16
F32 = jnp.float32


def attention_kernel(ctx_count, keep, q_ref, k_ref, v_ref, me_ref, o_ref):
    heads = q_ref.shape[1] // HD
    me = me_ref[0]
    rows = keep // 2
    for half in range(2):
        span = rows * (half + 1)
        q_rank = (lax.broadcasted_iota(jnp.int32, (rows, span), 0) + half * rows) * ctx_count + me
        slot = lax.broadcasted_iota(jnp.int32, (rows, span), 1) * ctx_count
        masks = [slot + c <= q_rank for c in range(ctx_count)]
        for h in range(heads):
            q = q_ref[pl.ds(half * rows, rows), pl.ds(h * HD, HD)]
            scores = []
            for c in range(ctx_count):
                s = lax.dot_general(
                    q, k_ref[c, pl.ds(0, span), :], (((1,), (1,)), ((), ())),
                    preferred_element_type=F32,
                ) * (HD ** -0.5)
                scores.append(jnp.where(masks[c], s, MASKED_SCORE))
            peak = functools.reduce(jnp.maximum, scores)
            peak = jnp.max(peak, axis=1, keepdims=True)
            total = jnp.zeros((rows, span), F32)
            mixed = jnp.zeros((rows, HD), F32)
            for c in range(ctx_count):
                w = jnp.exp(scores[c] - peak)
                total = total + w
                mixed = mixed + jnp.dot(
                    w.astype(BF16), v_ref[c, pl.ds(0, span), :], preferred_element_type=F32
                )
            total = jnp.sum(total, axis=1, keepdims=True)
            o_ref[pl.ds(half * rows, rows), pl.ds(h * HD, HD)] = (mixed / total).astype(BF16)


def attention(q, k, v, me, ctx_count, keep):
    return pl.pallas_call(
        functools.partial(attention_kernel, ctx_count, keep),
        out_shape=jax.ShapeDtypeStruct(q.shape, BF16),
        in_specs=[pl.BlockSpec(memory_space=pltpu.VMEM)] * 3
        + [pl.BlockSpec(memory_space=pltpu.SMEM)],
        out_specs=pl.BlockSpec(memory_space=pltpu.VMEM),
        compiler_params=pltpu.CompilerParams(vmem_limit_bytes=48 * 2**20),
        name="attention",
    )(q, k, v, me)


def one_hot(index, count, axis):
    shape = (count,) + index.shape if axis == 0 else index.shape + (count,)
    iota = lax.broadcasted_iota(jnp.int32, shape, 0 if axis == 0 else len(shape) - 1)
    target = index[None] if axis == 0 else index[..., None]
    return (iota == target).astype(BF16)


def shards(hidden, norm_gain, router_weight, query_weight, key_value_weight, out_weight, kept_rows):
    me = lax.axis_index("ctx")
    ctx_count = lax.axis_size("ctx")
    tp_count = lax.axis_size("tp")
    tp_index = lax.axis_index("tp")
    token_count, width = hidden.shape
    capacity = kept_rows.shape[1]
    keep = capacity // 2
    part = capacity // ctx_count
    heads = H // tp_count

    counts = jnp.sum((kept_rows < token_count).astype(jnp.int32), axis=1)
    starts = jnp.cumsum(counts) - counts
    ids = jnp.arange(ctx_count, dtype=jnp.int32)
    slots = jnp.arange(part, dtype=jnp.int32)

    first = (ids - starts[me]) % ctx_count
    send_index = first[:, None] + ctx_count * slots[None, :]
    own_rows = lax.dynamic_index_in_dim(kept_rows, me, 0, keepdims=False)
    hits = send_index.reshape(-1)[:, None] == jnp.arange(capacity, dtype=jnp.int32)[None, :]
    send_rows = jnp.sum(jnp.where(hits, own_rows[None, :], 0), axis=1)
    pick = one_hot(send_rows, token_count, 1)
    sent = jnp.dot(pick, hidden, preferred_element_type=F32).astype(BF16)
    got = lax.all_to_all(sent.reshape(ctx_count, part, width), "ctx", 0, 0).reshape(capacity, width)

    come_first = (me - starts) % ctx_count
    come_slot = (starts + come_first)[:, None] // ctx_count + slots[None, :]
    come_valid = come_first[:, None] + ctx_count * slots[None, :] < counts[:, None]
    place = jnp.where(come_valid, come_slot, keep).reshape(-1)
    compact = one_hot(place, keep, 0)
    kept = jnp.dot(compact, got, preferred_element_type=F32).astype(BF16)

    widened = kept.astype(F32)
    square_part = jnp.sum(widened * widened, axis=1)
    router_part = jnp.dot(kept, router_weight, preferred_element_type=F32)
    normed = (widened * norm_gain.astype(F32)).astype(BF16)

    pieces = []
    remainder = jnp.stack([square_part, router_part])
    for _ in range(3):
        piece = lax.reduce_precision(remainder, 8, 7)
        pieces.append(piece.astype(BF16))
        remainder = remainder - piece
    own_slot = (jnp.arange(tp_count) == tp_index)[:, None, None]
    stat_terms = jnp.where(own_slot, jnp.concatenate(pieces)[None], 0).reshape(6 * tp_count, keep)
    stat_terms = jnp.broadcast_to(stat_terms[None], (tp_count,) + stat_terms.shape)

    kv_terms = lax.dot_general(
        key_value_weight, normed, (((1,), (1,)), ((), ())), preferred_element_type=F32
    ).astype(BF16).reshape(2, KVH, HD, keep)
    group_of = [t * heads // (H // KVH) for t in range(tp_count)]
    kv_terms = jnp.stack([kv_terms[:, g] for g in group_of]).reshape(tp_count, 2 * HD, keep)
    kv_sums = lax.psum_scatter(
        jnp.concatenate([kv_terms, stat_terms], axis=1), "tp", scatter_dimension=0, tiled=False
    )
    q_terms = lax.dot_general(
        query_weight, normed, (((0,), (1,)), ((), ())), preferred_element_type=F32
    ).astype(BF16)
    q_sums = lax.psum_scatter(q_terms, "tp", scatter_dimension=0, tiled=True)

    stats = jnp.sum(kv_sums[2 * HD :].astype(F32).reshape(tp_count * 3, 2, keep), axis=0)
    inverse_rms = lax.rsqrt(stats[0] / D + EPSILON)
    router_logit = stats[1]
    key_values = (kv_sums[: 2 * HD].astype(F32) * inverse_rms[None, :]).astype(BF16).T
    key_values = lax.all_to_all(
        jnp.broadcast_to(key_values[None], (ctx_count,) + key_values.shape), "ctx", 0, 0
    )
    queries = (q_sums.astype(F32) * inverse_rms[None, :]).astype(BF16).T

    batches = 2
    size = heads // batches * HD
    weight = out_weight.reshape(tp_count, batches, size, width)
    projected = 0.0
    for b in range(batches):
        head_output = attention(
            queries[:, b * size : (b + 1) * size], key_values[:, :, :HD], key_values[:, :, HD:],
            me.reshape(1), ctx_count, keep,
        )
        gathered = lax.all_gather(head_output, "tp", axis=0, tiled=False)
        projected = projected + jnp.einsum(
            "tqe,tef->qf", gathered, weight[:, b], preferred_element_type=F32
        )
    row_update = (jax.nn.sigmoid(router_logit)[:, None] * projected).astype(BF16)

    back = lax.dot_general(
        compact, row_update, (((0,), (0,)), ((), ())), preferred_element_type=F32
    ).astype(BF16)
    home = lax.all_to_all(back.reshape(ctx_count, part, width), "ctx", 0, 0).reshape(capacity, width)
    return lax.dot_general(
        pick, home, (((0,), (0,)), ((), ())), preferred_element_type=F32
    ).astype(BF16)


def solution(mesh):
    return jax.shard_map(
        shards,
        mesh=mesh,
        in_specs=(
            P("ctx", "tp"),
            P("tp"),
            P("tp"),
            P("tp", None),
            P(None, "tp", None),
            P(None, "tp"),
            P(),
        ),
        out_specs=P("ctx", "tp"),
        check_vma=False,
    )
```
